512 devices in a mesh: dp: 8 (over y, core), expert: 64 (over x, z).
Axes of the slice: x: 4, y: 4, z: 16, core: 2. Of those that a mesh axis runs over, the one named last changes fastest.
Arguments:
- input_rows: bfloat16 [32768, 7168], P(('dp', 'expert')), may hold values from -6 to 6
- row_scales: float32 [32768, 56], P(('dp', 'expert')), may hold values from 0.25 to 4
- output_grad: bfloat16 [32768, 7168], P(('dp', 'expert')), may hold values from -6 to 6
- expert_ids: int32 [32768, 8], P(('dp', 'expert')), may hold values from 0 to 255, all different within a row; in each aligned block of 64 rows (0 to 63, 64 to 127, ...) at most 4 rows name the same one
- combine_weights: float32 [32768, 8], P(('dp', 'expert')), may hold values from 0.1 to 1
- gate_proj: bfloat16 [64, 7168, 256], P('expert', 'dp'), may hold values from -0.0625 to 0.0625
- up_proj: bfloat16 [64, 7168, 256], P('expert', 'dp'), may hold values from -0.0625 to 0.0625
- down_proj: bfloat16 [64, 256, 7168], P('expert', None, 'dp'), may hold values from -0.1875 to 0.1875
Outputs:
- input_grad: bfloat16 [32768, 7168], P(('dp', 'expert'))
The draws below stay inside these ranges and needn't reach their ends.
Inputs may be any that keep to these rules, and one draw needn't show every extreme that they name: `expert_ids`: each row names 8 different experts. Among the rows of one device no number appears more than 4 times, and some number appears exactly 4 times in the rows of some device.
All inputs are finite; a program needn't handle non-finite values.
Results may differ from the reference program's by a relative error of at most 0.034.
Values may be sent and summed in bfloat16 or wider, within the bound.
No kernel may reach another device: no remote copies, remote signals or barrier semaphores. Data moves between devices by JAX's collectives and lax.ppermute only.
A program may use at most 128 MiB of HBM per device.

```python
import math
import jax
import jax.numpy as jnp
import numpy as np
from jax import lax

D = 7168
HQ = 256
ROUTED = 256
TOP = 8
BLOCK = 128
TOK_DEV = 64
CAP = 4
HW = 1024
TOKENS = 32768
N_DP = 8
N_EXPERT = 64


def block_levels(rng, extent, split, least, top_value):
    factor_of, own = 1.0, jax.random.fold_in(rng, 6)
    for axis_at, parts in split:
        steps = jnp.exp(jax.random.uniform(jax.random.fold_in(own, axis_at), (parts,), jnp.float32, least / len(split), top_value / len(split)))
        factor_of = factor_of * jnp.repeat(steps, extent[axis_at] // parts).reshape([-1 if axis == axis_at else 1 for axis in range(len(extent))])
    return factor_of


def assign_block(own_key, own, number, rows, count, top, limit, skew):
    sequence = jax.random.permutation(own_key, count)
    packed, common = portions_of(count, rows * top, limit, skew, True), portions_of(count, rows * top, limit, skew, False)
    places = jnp.arange(count)

    def named(sizes, offset_by):
        used = int((sizes > 0).sum())
        fixed = max(1, used // 4)
        passed = fixed + (places - fixed + offset_by * (used - fixed)) % max(1, count - fixed)
        return jnp.zeros((count,), jnp.int32).at[sequence[jnp.where(places < fixed, places, passed)]].set(jnp.asarray(sizes, jnp.int32))

    sizes = jnp.where(number % 4 == 0, named(packed, number // 4), named(common, number - number // 4 - 1))
    mixed = jax.random.permutation(jax.random.fold_in(own, 3), count)
    donor, receiver = mixed[0:count // 2 * 2:2], mixed[1:count // 2 * 2:2]
    margin = jnp.minimum(sizes[donor] - 1, limit - sizes[receiver]) // 2
    margin = jnp.where((donor == sequence[0]) | (receiver == sequence[0]) | (sizes[receiver] == 0), 0, jnp.maximum(margin, 0))
    passed = jax.random.randint(jax.random.fold_in(own, 4), (count // 2,), 0, 1 << 20) % (margin + 1)
    sizes = sizes.at[donor].add(-passed).at[receiver].add(passed)
    members = jnp.searchsorted(jnp.cumsum(sizes), jnp.arange(rows * top), side="right").astype(jnp.int32)
    table = members.reshape(top, rows).T
    table = table[jax.random.permutation(jax.random.fold_in(own, 1), rows)]
    offset_by = jax.random.randint(jax.random.fold_in(own, 2), (rows, 1), 0, top)
    return jnp.take_along_axis(table, (jnp.arange(top)[None, :] + offset_by) % top, axis=1)


def portions_of(number_of, total, reach, slope, full):
    portions = [(1 << 20) // math.isqrt(grade ** slope) + 1 for grade in range(1, number_of + 1)]
    largest = reach if full else min(reach, max(-(-total // number_of), total * portions[0] // sum(portions)))
    least = 1 if total - largest >= number_of - 1 else 0
    counts, surplus = [largest] + [least] * (number_of - 1), total - largest - least * (number_of - 1)
    while surplus > 0:
        free = [i for i in range(1, number_of) if counts[i] < largest] or [i for i in range(1, number_of) if counts[i] < reach]
        pool, left = sum([portions[i] for i in free]), surplus
        for i in free:
            more = min(reach - counts[i], max(1, left * portions[i] // pool), surplus)
            counts[i] = counts[i] + more
            surplus = surplus - more
    return np.array(counts)


def bell_draw(rng, shape, deviation, limit, cuts=(), kind=jnp.bfloat16):
    drawn = deviation * jax.random.normal(rng, shape, jnp.float32)
    if cuts:
        drawn = drawn * block_levels(rng, shape, cuts, -0.22, 0.18)
    return jnp.clip(drawn, -limit, limit).astype(kind)


def setup_inputs(seed: int = 0) -> dict:
    keys = jax.random.split(jax.random.key(seed), 9)
    input_rows = bell_draw(keys[0], (TOKENS, D), 1.0, 6.0, ((0, 512),))
    row_scales = jnp.clip(jnp.exp(math.log(4.0) - 2.7725887 * jax.random.uniform(keys[1], (TOKENS, D // BLOCK), jnp.float32) ** block_levels(keys[1], (TOKENS, D // BLOCK), ((0, 512),), -0.2, 0.2)), 0.25, 4.0)
    output_grad = bell_draw(keys[2], (TOKENS, D), 1.0, 6.0, ((0, 512),))
    expert_ids_keys = jax.random.split(jax.random.fold_in(keys[3], 1), TOKENS // TOK_DEV)
    expert_ids_turns = jax.random.permutation(jax.random.fold_in(keys[3], 3), TOKENS // TOK_DEV)
    expert_ids = jax.vmap(lambda own, number: assign_block(jax.random.fold_in(keys[3], 2), own, number, TOK_DEV, ROUTED, TOP, CAP, 2))(expert_ids_keys, expert_ids_turns).reshape((TOKENS, TOP))
    combine_weights = jnp.clip(0.1 + 0.9 * jax.random.uniform(keys[4], (TOKENS, TOP), jnp.float32) ** block_levels(keys[4], (TOKENS, TOP), ((0, 512),), -0.2, 0.2), 0.1, 1.0)
    gate_proj = bell_draw(keys[5], (N_EXPERT, D, HQ), D ** -0.5, 0.0625, ((0, 64), (1, 8)))
    up_proj = bell_draw(keys[6], (N_EXPERT, D, HQ), D ** -0.5, 0.0625, ((0, 64), (1, 8)))
    down_proj = bell_draw(keys[7], (N_EXPERT, HQ, D), HW ** -0.5, 0.1875, ((0, 64), (2, 8)))
    return dict(input_rows=input_rows, row_scales=row_scales, output_grad=output_grad, expert_ids=expert_ids, combine_weights=combine_weights, gate_proj=gate_proj, up_proj=up_proj, down_proj=down_proj)


def reference(input_rows, row_scales, output_grad, expert_ids, combine_weights, gate_proj, up_proj, down_proj):
    devices_all = N_DP * N_EXPERT
    window = N_EXPERT // 4
    columns = D // N_DP
    rows_all = devices_all * CAP
    grid = expert_ids.reshape(devices_all, TOK_DEV, TOP)
    expert_range = jnp.arange(window, dtype=jnp.int32)
    member = jnp.sum((grid[:, :, :, None] == expert_range).astype(jnp.int32), axis=2)
    before = jnp.cumsum(member, axis=1) - member
    slot_range = jnp.arange(CAP, dtype=jnp.int32)
    hitting = member[:, :, :, None] * (before[:, :, :, None] == slot_range).astype(jnp.int32)
    local_ids = jnp.arange(TOK_DEV, dtype=jnp.int32)
    token_table = jnp.sum(hitting * local_ids[None, :, None, None], axis=1)
    token_table = token_table + (jnp.arange(devices_all, dtype=jnp.int32) * TOK_DEV)[:, None, None]
    alive_table = jnp.sum(hitting, axis=1)
    table = jnp.transpose(token_table, (1, 0, 2)).reshape(window, rows_all).astype(jnp.int32)
    alive_all = jnp.transpose(alive_table, (1, 0, 2)).reshape(window, rows_all).astype(jnp.float32)
    pick_weight = jnp.sum(combine_weights[:, :, None] * (expert_ids[:, :, None] == expert_range).astype(jnp.float32), axis=1)

    def rounded_sum(partial_value):
        return lax.optimization_barrier(partial_value.astype(jnp.bfloat16)).astype(jnp.float32).sum(0)

    def one_expert(carry, expert):
        indices = table[expert]
        alive = alive_all[expert]
        rows_q = input_rows[indices].astype(jnp.float32)
        scales = row_scales[indices]
        x_rows = (rows_q.reshape(rows_all, D // BLOCK, BLOCK) * scales[:, :, None]).reshape(rows_all, D).astype(jnp.bfloat16)
        grads = output_grad[indices]
        gate_full = jnp.concatenate([gate_proj[4 * expert + q] for q in range(4)], axis=1)
        up_full = jnp.concatenate([up_proj[4 * expert + q] for q in range(4)], axis=1)
        down_full = jnp.concatenate([down_proj[4 * expert + q] for q in range(4)], axis=0)
        x_blocks = x_rows.astype(jnp.float32).reshape(rows_all, N_DP, columns)
        g_blocks = grads.astype(jnp.float32).reshape(rows_all, N_DP, columns)
        gate_part = jnp.einsum("rnc,nch->nrh", x_blocks, gate_full.astype(jnp.float32).reshape(N_DP, columns, HW), precision=lax.Precision.HIGHEST)
        up_part = jnp.einsum("rnc,nch->nrh", x_blocks, up_full.astype(jnp.float32).reshape(N_DP, columns, HW), precision=lax.Precision.HIGHEST)
        hidden_part = jnp.einsum("rnc,hnc->nrh", g_blocks, down_full.astype(jnp.float32).reshape(HW, N_DP, columns), precision=lax.Precision.HIGHEST)
        gate_val = rounded_sum(gate_part)
        up_val = rounded_sum(up_part)
        hidden_grad = rounded_sum(hidden_part)
        sigmoid_gate = jax.nn.sigmoid(gate_val)
        gate_grad = (hidden_grad * up_val * sigmoid_gate * (1.0 + gate_val * (1.0 - sigmoid_gate))).astype(jnp.bfloat16)
        up_grad = (hidden_grad * gate_val * sigmoid_gate).astype(jnp.bfloat16)
        total = jnp.zeros((rows_all, D), jnp.float32)
        for quarter in range(4):
            lower = quarter * HQ
            part = jnp.dot(gate_grad[:, lower:lower + HQ], gate_full[:, lower:lower + HQ].T, preferred_element_type=jnp.float32)
            part = part + jnp.dot(up_grad[:, lower:lower + HQ], up_full[:, lower:lower + HQ].T, preferred_element_type=jnp.float32)
            total = total + part.astype(jnp.bfloat16).astype(jnp.float32)
        weight_rows = pick_weight[indices, expert] * alive
        carry = carry.at[indices].add(total * weight_rows[:, None])
        return carry, None

    result, unused = lax.scan(one_expert, jnp.zeros((TOKENS, D), jnp.float32), jnp.arange(window, dtype=jnp.int32))
    return result.astype(jnp.bfloat16)
```

```python
import jax
import jax.numpy as jnp
from jax import lax
from jax.sharding import Mesh, PartitionSpec as P

BLOCK = 128
CAP = 4
QUARTERS = 4
CHUNKS = 2

DP = ("y", "c")
EX = ("xh", "l")
bf16 = jnp.bfloat16
f32 = jnp.float32


def mm(left, right):
    return jnp.dot(left, right, preferred_element_type=f32)


def mm_t(left, right):
    return lax.dot_general(left, right, (((1,), (1,)), ((), ())), preferred_element_type=f32)


def one_hot_rows(source):
    count = source.shape[0]
    return (source[:, None] == jnp.arange(count, dtype=jnp.int32)[None, :]).astype(bf16)


def swiglu_grads(gate_val, up_val, hidden_grad):
    sigmoid_gate = jax.nn.sigmoid(gate_val)
    gate_grad = hidden_grad * up_val * sigmoid_gate * (1.0 + gate_val * (1.0 - sigmoid_gate))
    up_grad = hidden_grad * gate_val * sigmoid_gate
    return gate_grad.astype(bf16), up_grad.astype(bf16)


def per_device(
    input_rows, row_scales, output_grad, expert_ids, combine_weights, gate_proj, up_proj, down_proj
):
    tokens, width = input_rows.shape
    n_dp = lax.axis_size(DP)
    n_ex = lax.axis_size(EX)
    window = n_ex // QUARTERS
    cols = width // n_dp

    gate_all, up_all, down_all = (
        lax.all_gather(gate_proj[0], "l"),
        lax.all_gather(up_proj[0], "l"),
        lax.all_gather(down_proj[0], "l"),
    )

    hits = (expert_ids[:, :, None] == jnp.arange(window, dtype=jnp.int32)).astype(f32)
    member = jnp.sum(hits, axis=1)
    pick_weight = jnp.sum(combine_weights[:, :, None] * hits, axis=1)
    before = jnp.cumsum(member, axis=0) - member
    select = member[:, :, None] * (
        before[:, :, None] == jnp.arange(CAP, dtype=f32)
    ).astype(f32)
    weighting = (select * pick_weight[:, :, None]).reshape(tokens, window * CAP)
    select = select.reshape(tokens, window * CAP).T.astype(bf16)

    x = (input_rows.astype(f32) * jnp.repeat(row_scales, BLOCK, axis=1)).astype(bf16)

    def picked(array):
        return jnp.stack(
            [
                mm(select, array[:, d * cols : (d + 1) * cols]).astype(bf16)
                for d in range(n_dp)
            ]
        )

    sent = jnp.concatenate([picked(x), picked(output_grad)], axis=1)
    got = lax.all_to_all(sent, DP, split_axis=0, concat_axis=0, tiled=True)

    part_dp = n_dp // CHUNKS
    rows = n_ex * part_dp
    both = 2 * rows
    place = jnp.arange(both, dtype=jnp.int32)
    dest, kind, src = place // (2 * part_dp), place // part_dp % 2, place % part_dp
    to_send = one_hot_rows(src * (2 * n_ex) + kind * n_ex + dest)
    kind2, rest = place // rows, place % rows
    to_split = one_hot_rows(rest // part_dp * (2 * part_dp) + kind2 * part_dp + rest % part_dp)
    place3 = jnp.arange(rows, dtype=jnp.int32)
    to_slots = one_hot_rows(place3 % n_ex * part_dp + place3 // n_ex)

    def forward(chunk):
        mine = got[chunk * part_dp : (chunk + 1) * part_dp].reshape(both, cols)
        mine = mm(to_send, mine).astype(bf16).reshape(n_ex, 2 * part_dp, cols)
        there = lax.all_to_all(mine, EX, split_axis=0, concat_axis=0, tiled=True)
        return there.reshape(both, cols)

    def hidden_parts(there):
        split = mm(to_split, there).astype(bf16)
        x_rows, grads = split[:rows], split[rows:]
        parts = [mm(x_rows, gate_all[q]).astype(bf16) for q in range(QUARTERS)]
        parts += [mm(x_rows, up_all[q]).astype(bf16) for q in range(QUARTERS)]
        parts += [mm_t(grads, down_all[q]).astype(bf16) for q in range(QUARTERS)]
        return jnp.concatenate(parts, axis=1)

    def activations(parts):
        summed = lax.psum_scatter(parts, DP, scatter_dimension=0, tiled=True).astype(f32)
        hidden = summed.shape[1] // 3
        grads = swiglu_grads(
            summed[:, :hidden], summed[:, hidden : 2 * hidden], summed[:, 2 * hidden :]
        )
        return lax.all_gather(jnp.concatenate(grads, axis=1), DP, axis=0, tiled=True)

    def backward(acts):
        hq = gate_all.shape[2]
        part = jnp.zeros((rows, cols), f32)
        for q in range(QUARTERS):
            part = part + mm_t(acts[:, q * hq : (q + 1) * hq], gate_all[q])
            part = part + mm_t(acts[:, (QUARTERS + q) * hq : (QUARTERS + q + 1) * hq], up_all[q])
        part = part.astype(bf16).reshape(n_ex, part_dp, cols)
        back = lax.all_to_all(part, EX, split_axis=0, concat_axis=0, tiled=True)
        back = mm(to_slots, back.reshape(rows, cols)).astype(bf16)
        return back.reshape(part_dp, n_ex, cols)

    arrived = [forward(k) for k in range(CHUNKS)]
    acts = [activations(hidden_parts(a)) for a in arrived]
    back = jnp.concatenate([backward(a) for a in acts], axis=0)
    home = lax.all_to_all(back, DP, split_axis=0, concat_axis=0, tiled=True)
    high = weighting.astype(bf16)
    low = (weighting - high.astype(f32)).astype(bf16)
    return jnp.concatenate(
        [(mm(high, home[d]) + mm(low, home[d])).astype(bf16) for d in range(n_dp)], axis=1
    )


def solution(mesh):
    n_dp, n_ex = mesh.devices.shape
    fine = Mesh(
        mesh.devices.reshape(n_dp // 2, 2, n_ex // QUARTERS, QUARTERS), ("y", "c", "xh", "l")
    )
    tok = P(("y", "c", "xh", "l"), None)
    return jax.shard_map(
        per_device,
        mesh=fine,
        in_specs=(tok, tok, tok, tok, tok, P(EX, DP, None), P(EX, DP, None), P(EX, None, DP)),
        out_specs=tok,
        check_vma=False,
    )
```

```python
import jax
import jax.numpy as jnp
from jax import lax
from jax.experimental import pallas as pl
from jax.experimental.pallas import tpu as pltpu
from jax.sharding import Mesh, PartitionSpec as P

BLOCK = 128
CAP = 4
QUARTERS = 4

PLANE = ("y", "x", "h", "l")
bf16 = jnp.bfloat16
f32 = jnp.float32


def mm(left, right):
    return jnp.dot(left, right, preferred_element_type=f32)


def mm_t(left, right):
    return lax.dot_general(left, right, (((1,), (1,)), ((), ())), preferred_element_type=f32)


def shift(array, axis, k):
    n = lax.axis_size(axis)
    return lax.ppermute(array, axis, [(i, (i + k) % n) for i in range(n)])


def swiglu_grads(gate_val, up_val, hidden_grad):
    sigmoid_gate = jax.nn.sigmoid(gate_val)
    gate_grad = hidden_grad * up_val * sigmoid_gate * (1.0 + gate_val * (1.0 - sigmoid_gate))
    up_grad = hidden_grad * gate_val * sigmoid_gate
    return gate_grad.astype(bf16), up_grad.astype(bf16)


def weight_copies(core, own, other, held, sems, kinds):
    return [
        [
            pltpu.make_async_copy(
                piece.at[:, kind], held.at[half, kind, k], sems.at[side, kind, k]
            )
            for side, (half, pieces) in enumerate(((core, own), (1 - core, other)))
            for k, piece in enumerate(pieces)
        ]
        for kind in range(kinds)
    ]


def forward_kernel(place, x_ref, g_ref, *refs):
    own, other = refs[:QUARTERS], refs[QUARTERS : 2 * QUARTERS]
    out_ref, held, sems = refs[2 * QUARTERS :]
    copies = weight_copies(place[1], own, other, held, sems, 3)
    for group in copies:
        for copy in group:
            copy.start()
    n_y, rows, _ = out_ref.shape
    _, _, n_k, n_m, units, cols = held.shape
    span = n_m * units
    for kind, rows_ref in enumerate((x_ref, x_ref, g_ref)):
        for copy in copies[kind]:
            copy.wait()
        for k in range(n_k):
            part = mm_t(rows_ref[:, :cols], held[0, kind, k].reshape(span, cols))
            part = part + mm_t(rows_ref[:, cols:], held[1, kind, k].reshape(span, cols))
            at = (kind * n_k + k) * span
            out_ref[:, :, at : at + span] = part.astype(bf16).reshape(n_y, rows, span)


def backward_kernel(place, *refs):
    acts = refs[:QUARTERS]
    own, other = refs[QUARTERS : 2 * QUARTERS], refs[2 * QUARTERS : 3 * QUARTERS]
    out_ref, held, acts_held, sems, act_sems = refs[3 * QUARTERS :]
    copies = weight_copies(place[1], own, other, held, sems, 2)
    act_copies = [
        pltpu.make_async_copy(act, acts_held.at[(place[0] - k + QUARTERS) % QUARTERS], act_sems.at[k])
        for k, act in enumerate(acts)
    ]
    for copy in act_copies:
        copy.start()
    for group in copies:
        for copy in group:
            copy.start()
    for copy in act_copies:
        copy.wait()
    for group in copies:
        for copy in group:
            copy.wait()
    n_y, rows, width = acts_held.shape
    _, _, n_k, n_m, units, cols = held.shape
    hidden = n_k * n_m * units
    both = acts_held[...].reshape(n_y * rows, width)
    for half in range(2):
        part = mm(both[:, :hidden], held[half, 0].reshape(hidden, cols))
        part = part + mm(both[:, hidden:], held[half, 1].reshape(hidden, cols))
        out_ref[:, half * cols : (half + 1) * cols] = part.astype(bf16)


ANY = pl.BlockSpec(memory_space=pl.ANY)
VMEM = pl.BlockSpec(memory_space=pltpu.VMEM)
SMEM = pl.BlockSpec(memory_space=pltpu.SMEM)
PARAMS = pltpu.CompilerParams(vmem_limit_bytes=40 * 1024 * 1024)


def forward_parts(place, x_rows, g_rows, own, other, n_y):
    total, width = x_rows.shape
    n_m, _, units, cols = own[0].shape
    hidden = QUARTERS * n_m * units
    return pl.pallas_call(
        forward_kernel,
        out_shape=jax.ShapeDtypeStruct((n_y, total // n_y, 3 * hidden), bf16),
        in_specs=[SMEM, VMEM, VMEM] + [ANY] * (2 * QUARTERS),
        out_specs=VMEM,
        scratch_shapes=[
            pltpu.VMEM((2, 3, QUARTERS, n_m, units, cols), bf16),
            pltpu.SemaphoreType.DMA((2, 3, QUARTERS)),
        ],
        compiler_params=PARAMS,
        cost_estimate=pl.CostEstimate(
            flops=6 * total * width * hidden,
            bytes_accessed=6 * width * hidden,
            transcendentals=0,
        ),
    )(place, x_rows, g_rows, *own, *other)


def backward_parts(place, acts, own, other):
    rows, double = acts[0].shape
    n_m, _, units, cols = own[0].shape
    total = QUARTERS * rows
    return pl.pallas_call(
        backward_kernel,
        out_shape=jax.ShapeDtypeStruct((total, 2 * cols), bf16),
        in_specs=[SMEM] + [ANY] * (3 * QUARTERS),
        out_specs=VMEM,
        scratch_shapes=[
            pltpu.VMEM((2, 2, QUARTERS, n_m, units, cols), bf16),
            pltpu.VMEM((QUARTERS, rows, double), bf16),
            pltpu.SemaphoreType.DMA((2, 2, QUARTERS)),
            pltpu.SemaphoreType.DMA((QUARTERS,)),
        ],
        compiler_params=PARAMS,
        cost_estimate=pl.CostEstimate(
            flops=4 * total * double * cols,
            bytes_accessed=4 * double * cols,
            transcendentals=0,
        ),
    )(place, *acts, *own, *other)


def moved_weights(gate, up, down):
    x, l = lax.axis_index("x"), lax.axis_index("l")
    hq, cols = down.shape
    units = hq // QUARTERS
    joined = jnp.stack([gate.T, up.T, down]).reshape(3, QUARTERS, units, cols).transpose(1, 0, 2, 3)

    def pick(array, index):
        return lax.dynamic_index_in_dim(array, index % QUARTERS, 0, keepdims=False)

    along_x = jnp.stack(
        [pick(joined, x)] + [shift(pick(joined, x + k), "x", k) for k in range(1, QUARTERS)]
    )
    along_l = jnp.stack(
        [pick(along_x, x - l + QUARTERS)]
        + [shift(pick(along_x, x - l - m + 2 * QUARTERS), "l", m) for m in range(1, QUARTERS)]
    )
    own = [along_l] + [shift(along_l, "x", k) for k in range(1, QUARTERS)]
    return own, [shift(piece, "c", 1) for piece in own]


def per_device(
    input_rows, row_scales, output_grad, expert_ids, combine_weights, gate_proj, up_proj, down_proj
):
    tokens, width = input_rows.shape
    n_y, n_ex = lax.axis_size("y"), lax.axis_size(("x", "h", "l"))
    window = n_ex // QUARTERS
    cols = width // n_y

    hits = (expert_ids[:, :, None] == jnp.arange(window, dtype=jnp.int32)).astype(f32)
    member = jnp.sum(hits, axis=1)
    pick_weight = jnp.sum(combine_weights[:, :, None] * hits, axis=1)
    before = jnp.cumsum(member, axis=0) - member
    select = member[:, :, None] * (
        before[:, :, None] == jnp.arange(CAP, dtype=f32)
    ).astype(f32)

    def by_device(array):
        split = array.reshape(tokens, QUARTERS, window // QUARTERS, CAP)
        return split.transpose(0, 3, 2, 1).reshape(tokens, n_ex)

    weighting = by_device(select * pick_weight[:, :, None])
    select = by_device(select).T.astype(bf16)

    x = (input_rows.astype(f32) * jnp.repeat(row_scales, BLOCK, axis=1)).astype(bf16)

    def picked(array, y):
        return mm(select, array[:, y * cols : (y + 1) * cols]).astype(bf16)

    sent = jnp.stack(
        [jnp.stack([picked(x, y), picked(output_grad, y)], axis=1) for y in range(n_y)]
    ).reshape(n_y * n_ex, 2, cols)
    there = lax.all_to_all(sent, PLANE, split_axis=0, concat_axis=0, tiled=True)

    own, other = moved_weights(gate_proj[0], up_proj[0], down_proj[0])
    place = jnp.stack([lax.axis_index("y"), lax.axis_index("c")]).astype(jnp.int32)
    parts = forward_parts(place, there[:, 0], there[:, 1], own, other, n_y)
    parts = lax.all_to_all(parts, "y", split_axis=0, concat_axis=0, tiled=True)
    summed = jnp.sum(parts.astype(f32), axis=0)
    hidden = summed.shape[1] // 3
    acts = jnp.concatenate(
        swiglu_grads(
            summed[:, :hidden], summed[:, hidden : 2 * hidden], summed[:, 2 * hidden :]
        ),
        axis=1,
    )
    acts = [acts] + [shift(acts, "y", k) for k in range(1, QUARTERS)]
    part = backward_parts(place, acts, own, other)
    home = lax.all_to_all(
        part.reshape(n_y * n_ex, 1, cols), PLANE, split_axis=0, concat_axis=0, tiled=True
    ).reshape(n_y, n_ex, cols)
    high = weighting.astype(bf16)
    low = (weighting - high.astype(f32)).astype(bf16)
    return jnp.concatenate(
        [(mm(high, home[y]) + mm(low, home[y])).astype(bf16) for y in range(n_y)], axis=1
    )


def solution(mesh):
    n_dp, n_ex = mesh.devices.shape
    fine = Mesh(
        mesh.devices.reshape(n_dp // 2, 2, QUARTERS, n_ex // QUARTERS**2, QUARTERS),
        ("y", "c", "x", "h", "l"),
    )
    tok = P(("y", "c", "x", "h", "l"), None)
    ex, dp = ("x", "h", "l"), ("y", "c")
    return jax.shard_map(
        per_device,
        mesh=fine,
        in_specs=(tok, tok, tok, tok, tok, P(ex, dp, None), P(ex, dp, None), P(ex, None, dp)),
        out_specs=tok,
        check_vma=False,
    )
```

```python
import jax
import jax.numpy as jnp
from jax import lax
from jax.experimental import pallas as pl
from jax.experimental.pallas import tpu as pltpu
from jax.sharding import Mesh, PartitionSpec as P

BLOCK = 128
CAP = 4
QUARTERS = 4

PLANE = ("y", "x", "h", "l")
bf16 = jnp.bfloat16
f32 = jnp.float32


def mm(left, right):
    return jnp.dot(left, right, preferred_element_type=f32)


def mm_t(left, right):
    return lax.dot_general(left, right, (((1,), (1,)), ((), ())), preferred_element_type=f32)


def shift(array, axis, k):
    n = lax.axis_size(axis)
    return lax.ppermute(array, axis, [(i, (i + k) % n) for i in range(n)])


def swiglu_grads(gate_val, up_val, hidden_grad):
    sigmoid_gate = jax.nn.sigmoid(gate_val)
    gate_grad = hidden_grad * up_val * sigmoid_gate * (1.0 + gate_val * (1.0 - sigmoid_gate))
    up_grad = hidden_grad * gate_val * sigmoid_gate
    return gate_grad.astype(bf16), up_grad.astype(bf16)


def weight_copies(core, own, other, held, sems, kinds):
    return [
        [
            pltpu.make_async_copy(
                piece.at[:, kind], held.at[half, kind, k], sems.at[side, kind, k]
            )
            for side, (half, pieces) in enumerate(((core, own), (1 - core, other)))
            for k, piece in enumerate(pieces)
        ]
        for kind in range(kinds)
    ]


def forward_kernel(place, x_ref, g_ref, *refs):
    own, other = refs[:QUARTERS], refs[QUARTERS : 2 * QUARTERS]
    out_ref, held, sems = refs[2 * QUARTERS :]
    copies = weight_copies(place[1], own, other, held, sems, 3)
    for group in copies:
        for copy in group:
            copy.start()
    n_y, rows, _ = out_ref.shape
    _, _, n_k, n_m, units, cols = held.shape
    span = n_m * units
    for kind, rows_ref in enumerate((x_ref, x_ref, g_ref)):
        for copy in copies[kind]:
            copy.wait()
        for k in range(n_k):
            part = mm_t(rows_ref[:, :cols], held[0, kind, k].reshape(span, cols))
            part = part + mm_t(rows_ref[:, cols:], held[1, kind, k].reshape(span, cols))
            at = (kind * n_k + k) * span
            out_ref[:, :, at : at + span] = part.astype(bf16).reshape(n_y, rows, span)


def backward_kernel(place, *refs):
    acts = refs[:QUARTERS]
    own, other = refs[QUARTERS : 2 * QUARTERS], refs[2 * QUARTERS : 3 * QUARTERS]
    out_ref, held, acts_held, sems, act_sems = refs[3 * QUARTERS :]
    copies = weight_copies(place[1], own, other, held, sems, 2)
    act_copies = [
        pltpu.make_async_copy(act, acts_held.at[(place[0] - k + QUARTERS) % QUARTERS], act_sems.at[k])
        for k, act in enumerate(acts)
    ]
    for copy in act_copies:
        copy.start()
    for group in copies:
        for copy in group:
            copy.start()
    for copy in act_copies:
        copy.wait()
    for group in copies:
        for copy in group:
            copy.wait()
    n_y, rows, width = acts_held.shape
    _, _, n_k, n_m, units, cols = held.shape
    hidden = n_k * n_m * units
    both = acts_held[...].reshape(n_y * rows, width)
    for half in range(2):
        part = mm(both[:, :hidden], held[half, 0].reshape(hidden, cols))
        part = part + mm(both[:, hidden:], held[half, 1].reshape(hidden, cols))
        out_ref[:, half * cols : (half + 1) * cols] = part.astype(bf16)


ANY = pl.BlockSpec(memory_space=pl.ANY)
VMEM = pl.BlockSpec(memory_space=pltpu.VMEM)
SMEM = pl.BlockSpec(memory_space=pltpu.SMEM)
PARAMS = pltpu.CompilerParams(vmem_limit_bytes=40 * 1024 * 1024)


def forward_parts(place, x_rows, g_rows, own, other, n_y):
    total, width = x_rows.shape
    n_m, _, units, cols = own[0].shape
    hidden = QUARTERS * n_m * units
    return pl.pallas_call(
        forward_kernel,
        out_shape=jax.ShapeDtypeStruct((n_y, total // n_y, 3 * hidden), bf16),
        in_specs=[SMEM, VMEM, VMEM] + [ANY] * (2 * QUARTERS),
        out_specs=VMEM,
        scratch_shapes=[
            pltpu.VMEM((2, 3, QUARTERS, n_m, units, cols), bf16),
            pltpu.SemaphoreType.DMA((2, 3, QUARTERS)),
        ],
        compiler_params=PARAMS,
        cost_estimate=pl.CostEstimate(
            flops=6 * total * width * hidden,
            bytes_accessed=6 * width * hidden,
            transcendentals=0,
        ),
    )(place, x_rows, g_rows, *own, *other)


def backward_parts(place, acts, own, other):
    rows, double = acts[0].shape
    n_m, _, units, cols = own[0].shape
    total = QUARTERS * rows
    return pl.pallas_call(
        backward_kernel,
        out_shape=jax.ShapeDtypeStruct((total, 2 * cols), bf16),
        in_specs=[SMEM] + [ANY] * (3 * QUARTERS),
        out_specs=VMEM,
        scratch_shapes=[
            pltpu.VMEM((2, 2, QUARTERS, n_m, units, cols), bf16),
            pltpu.VMEM((QUARTERS, rows, double), bf16),
            pltpu.SemaphoreType.DMA((2, 2, QUARTERS)),
            pltpu.SemaphoreType.DMA((QUARTERS,)),
        ],
        compiler_params=PARAMS,
        cost_estimate=pl.CostEstimate(
            flops=4 * total * double * cols,
            bytes_accessed=4 * double * cols,
            transcendentals=0,
        ),
    )(place, *acts, *own, *other)


def moved_weights(gate, up, down):
    x, l = lax.axis_index("x"), lax.axis_index("l")
    hq, cols = down.shape
    units = hq // QUARTERS
    joined = jnp.stack([gate.T, up.T, down]).reshape(3, QUARTERS, units, cols).transpose(1, 0, 2, 3)

    def pick(array, index):
        return lax.dynamic_index_in_dim(array, index % QUARTERS, 0, keepdims=False)

    along_x = jnp.stack(
        [pick(joined, x)] + [shift(pick(joined, x + k), "x", k) for k in range(1, QUARTERS)]
    )
    along_l = jnp.stack(
        [pick(along_x, x - l + QUARTERS)]
        + [shift(pick(along_x, x - l - m + 2 * QUARTERS), "l", m) for m in range(1, QUARTERS)]
    )
    return along_l


def spread_weights(piece):
    own = [piece] + [shift(piece, "x", k) for k in range(1, QUARTERS)]
    return own, [shift(piece, "c", 1) for piece in own]


def per_device(
    input_rows, row_scales, output_grad, expert_ids, combine_weights, gate_proj, up_proj, down_proj
):
    tokens, width = input_rows.shape
    n_y, n_ex = lax.axis_size("y"), lax.axis_size(("x", "h", "l"))
    window = n_ex // QUARTERS
    cols = width // n_y

    hits = (expert_ids[:, :, None] == jnp.arange(window, dtype=jnp.int32)).astype(f32)
    member = jnp.sum(hits, axis=1)
    pick_weight = jnp.sum(combine_weights[:, :, None] * hits, axis=1)
    before = jnp.cumsum(member, axis=0) - member
    select = member[:, :, None] * (
        before[:, :, None] == jnp.arange(CAP, dtype=f32)
    ).astype(f32)

    def by_device(array):
        split = array.reshape(tokens, QUARTERS, window // QUARTERS, CAP)
        return split.transpose(0, 3, 2, 1).reshape(tokens, n_ex)

    weighting = by_device(select * pick_weight[:, :, None])
    select = by_device(select).T.astype(bf16)

    x = (input_rows.astype(f32) * jnp.repeat(row_scales, BLOCK, axis=1)).astype(bf16)

    def picked(array, y):
        return mm(select, array[:, y * cols : (y + 1) * cols]).astype(bf16)

    sent = jnp.stack(
        [jnp.stack([picked(x, y), picked(output_grad, y)], axis=1) for y in range(n_y)]
    ).reshape(n_y * n_ex, 2, cols)
    piece = moved_weights(gate_proj[0], up_proj[0], down_proj[0])
    sent, piece = lax.optimization_barrier((sent, piece))
    there = lax.all_to_all(sent, PLANE, split_axis=0, concat_axis=0, tiled=True)

    own, other = spread_weights(piece)
    place = jnp.stack([lax.axis_index("y"), lax.axis_index("c")]).astype(jnp.int32)
    parts = forward_parts(place, there[:, 0], there[:, 1], own, other, n_y)
    parts = lax.all_to_all(parts, "y", split_axis=0, concat_axis=0, tiled=True)
    summed = jnp.sum(parts.astype(f32), axis=0)
    hidden = summed.shape[1] // 3
    acts = jnp.concatenate(
        swiglu_grads(
            summed[:, :hidden], summed[:, hidden : 2 * hidden], summed[:, 2 * hidden :]
        ),
        axis=1,
    )
    acts = [acts] + [shift(acts, "y", k) for k in range(1, QUARTERS)]
    part = backward_parts(place, acts, own, other)
    home = lax.all_to_all(
        part.reshape(n_y * n_ex, 1, cols), PLANE, split_axis=0, concat_axis=0, tiled=True
    ).reshape(n_y, n_ex, cols)
    high = weighting.astype(bf16)
    low = (weighting - high.astype(f32)).astype(bf16)
    return jnp.concatenate(
        [(mm(high, home[y]) + mm(low, home[y])).astype(bf16) for y in range(n_y)], axis=1
    )


def solution(mesh):
    n_dp, n_ex = mesh.devices.shape
    fine = Mesh(
        mesh.devices.reshape(n_dp // 2, 2, QUARTERS, n_ex // QUARTERS**2, QUARTERS),
        ("y", "c", "x", "h", "l"),
    )
    tok = P(("y", "c", "x", "h", "l"), None)
    ex, dp = ("x", "h", "l"), ("y", "c")
    return jax.shard_map(
        per_device,
        mesh=fine,
        in_specs=(tok, tok, tok, tok, tok, P(ex, dp, None), P(ex, dp, None), P(ex, None, dp)),
        out_specs=tok,
        check_vma=False,
    )
```

```python
import jax
import jax.numpy as jnp
from jax import lax
from jax.experimental import pallas as pl
from jax.experimental.pallas import tpu as pltpu
from jax.sharding import Mesh, PartitionSpec as P

BLOCK = 128
CAP = 4
QUARTERS = 4

PARTS = 1
EX = ("x", "h", "l")
bf16 = jnp.bfloat16
f32 = jnp.float32


def mm(left, right):
    return jnp.dot(left, right, preferred_element_type=f32)


def mm_t(left, right):
    return lax.dot_general(left, right, (((1,), (1,)), ((), ())), preferred_element_type=f32)


def shift(array, axis, k):
    n = lax.axis_size(axis)
    return lax.ppermute(array, axis, [(i, (i + k) % n) for i in range(n)])


def swiglu_grads(gate_val, up_val, hidden_grad):
    sigmoid_gate = jax.nn.sigmoid(gate_val)
    gate_grad = hidden_grad * up_val * sigmoid_gate * (1.0 + gate_val * (1.0 - sigmoid_gate))
    up_grad = hidden_grad * gate_val * sigmoid_gate
    return gate_grad.astype(bf16), up_grad.astype(bf16)


def weight_copies(core, pieces, held, sems, kinds):
    parts = len(pieces) // 2
    return [
        [
            pltpu.make_async_copy(
                piece.at[:, :, kind],
                held.at[core if n < parts else 1 - core, kind, n % parts],
                sems.at[kind, n],
            )
            for n, piece in enumerate(pieces)
        ]
        for kind in range(kinds)
    ]


def forward_kernel(place, x_ref, g_ref, *refs):
    pieces = refs[: 2 * PARTS]
    out_ref, held, sems = refs[2 * PARTS :]
    copies = weight_copies(place[1], pieces, held, sems, 3)
    for group in copies:
        for copy in group:
            copy.start()
    n_y, rows, _ = out_ref.shape
    _, _, n_p, n_k, n_m, units, cols = held.shape
    span = 2 * n_m * units
    for kind, rows_ref in enumerate((x_ref, x_ref, g_ref)):
        for copy in copies[kind]:
            copy.wait()
        for block in range(n_p * n_k // 2):
            p, k = block // (n_k // 2), block % (n_k // 2) * 2
            part = mm_t(rows_ref[:, :cols], held[0, kind, p, k : k + 2].reshape(span, cols))
            part = part + mm_t(rows_ref[:, cols:], held[1, kind, p, k : k + 2].reshape(span, cols))
            at = (kind * (n_p * n_k // 2) + block) * span
            part = part.astype(bf16).reshape(n_y, rows, span)
            for y in range(n_y):
                out_ref[(y - place[0] + n_y) % n_y, :, at : at + span] = part[y]


def backward_kernel(place, *refs):
    acts, pieces = refs[:QUARTERS], refs[QUARTERS : QUARTERS + 2 * PARTS]
    out_ref, held, acts_held, sems, act_sems = refs[QUARTERS + 2 * PARTS :]
    copies = weight_copies(place[1], pieces, held, sems, 2)
    act_copies = [
        pltpu.make_async_copy(act, acts_held.at[(place[0] - k + QUARTERS) % QUARTERS], act_sems.at[k])
        for k, act in enumerate(acts)
    ]
    for copy in act_copies:
        copy.start()
    for group in copies:
        for copy in group:
            copy.start()
    for copy in act_copies:
        copy.wait()
    for group in copies:
        for copy in group:
            copy.wait()
    n_y, rows, width = acts_held.shape
    _, _, n_p, n_k, n_m, units, cols = held.shape
    hidden = n_p * n_k * n_m * units
    both = acts_held[...].reshape(n_y * rows, width)
    for half in range(2):
        part = mm(both[:, :hidden], held[half, 0].reshape(hidden, cols))
        part = part + mm(both[:, hidden:], held[half, 1].reshape(hidden, cols))
        out_ref[:, half * cols : (half + 1) * cols] = part.astype(bf16)


ANY = pl.BlockSpec(memory_space=pl.ANY)
VMEM = pl.BlockSpec(memory_space=pltpu.VMEM)
SMEM = pl.BlockSpec(memory_space=pltpu.SMEM)
PARAMS = pltpu.CompilerParams(vmem_limit_bytes=40 * 1024 * 1024)


def forward_parts(place, x_rows, g_rows, pieces, n_y):
    total, width = x_rows.shape
    n_k, n_m, _, units, cols = pieces[0].shape
    hidden = PARTS * n_k * n_m * units
    return pl.pallas_call(
        forward_kernel,
        out_shape=jax.ShapeDtypeStruct((n_y, total // n_y, 3 * hidden), bf16),
        in_specs=[SMEM, VMEM, VMEM] + [ANY] * (2 * PARTS),
        out_specs=VMEM,
        scratch_shapes=[
            pltpu.VMEM((2, 3, PARTS, n_k, n_m, units, cols), bf16),
            pltpu.SemaphoreType.DMA((3, 2 * PARTS)),
        ],
        compiler_params=PARAMS,
        cost_estimate=pl.CostEstimate(
            flops=6 * total * width * hidden,
            bytes_accessed=6 * width * hidden,
            transcendentals=0,
        ),
    )(place, x_rows, g_rows, *pieces)


def backward_parts(place, acts, pieces):
    rows, double = acts[0].shape
    n_k, n_m, _, units, cols = pieces[0].shape
    total = QUARTERS * rows
    return pl.pallas_call(
        backward_kernel,
        out_shape=jax.ShapeDtypeStruct((total, 2 * cols), bf16),
        in_specs=[SMEM] + [ANY] * (QUARTERS + 2 * PARTS),
        out_specs=VMEM,
        scratch_shapes=[
            pltpu.VMEM((2, 2, PARTS, n_k, n_m, units, cols), bf16),
            pltpu.VMEM((QUARTERS, rows, double), bf16),
            pltpu.SemaphoreType.DMA((2, 2 * PARTS)),
            pltpu.SemaphoreType.DMA((QUARTERS,)),
        ],
        compiler_params=PARAMS,
        cost_estimate=pl.CostEstimate(
            flops=4 * total * double * cols,
            bytes_accessed=4 * double * cols,
            transcendentals=0,
        ),
    )(place, *acts, *pieces)


def combine_kernel(high_ref, low_ref, home_ref, out_ref):
    cols = home_ref.shape[2]
    for y in range(home_ref.shape[0]):
        total = mm(high_ref[...], home_ref[y]) + mm(low_ref[...], home_ref[y])
        out_ref[:, y * cols : (y + 1) * cols] = total.astype(bf16)


def combined(high, low, home):
    n_y, slots, cols = home.shape
    tokens = high.shape[0]
    return pl.pallas_call(
        combine_kernel,
        out_shape=jax.ShapeDtypeStruct((tokens, n_y * cols), bf16),
        in_specs=[VMEM] * 3,
        out_specs=VMEM,
        compiler_params=PARAMS,
        cost_estimate=pl.CostEstimate(
            flops=4 * tokens * slots * n_y * cols,
            bytes_accessed=4 * slots * n_y * cols,
            transcendentals=0,
        ),
    )(high, low, home)


def pick(array, index):
    return lax.dynamic_index_in_dim(array, index % QUARTERS, 0, keepdims=False)


def weights_along_x(joined):
    x = lax.axis_index("x")
    return jnp.stack(
        [pick(joined, x)] + [shift(pick(joined, x + k), "x", k) for k in range(1, QUARTERS)]
    )


def weights_along_l(along_x):
    x, l = lax.axis_index("x"), lax.axis_index("l")
    return jnp.stack(
        [pick(along_x, x - l + QUARTERS)]
        + [shift(pick(along_x, x - l - m + 2 * QUARTERS), "l", m) for m in range(1, QUARTERS)]
    )


def weights_spread(along_l):
    return lax.all_gather(along_l, "x")


def one_hot_rows(source):
    count = source.shape[0]
    return (source[:, None] == jnp.arange(count, dtype=jnp.int32)[None, :]).astype(bf16)


def per_device(
    input_rows, row_scales, output_grad, expert_ids, combine_weights, gate_proj, up_proj, down_proj
):
    tokens, width = input_rows.shape
    n_y, n_ex = lax.axis_size("y"), lax.axis_size(EX)
    window = n_ex // QUARTERS
    cols = width // n_y

    hits = (expert_ids[:, :, None] == jnp.arange(window, dtype=jnp.int32)).astype(f32)
    member = jnp.sum(hits, axis=1)
    pick_weight = jnp.sum(combine_weights[:, :, None] * hits, axis=1)
    before = jnp.cumsum(member, axis=0) - member
    select = member[:, :, None] * (
        before[:, :, None] == jnp.arange(CAP, dtype=f32)
    ).astype(f32)

    def by_device(array):
        split = array.reshape(tokens, QUARTERS, window // QUARTERS, CAP)
        return split.transpose(0, 3, 2, 1).reshape(tokens, n_ex)

    weighting = by_device(select * pick_weight[:, :, None])
    select = by_device(select).T.astype(bf16)

    x = (input_rows.astype(f32) * jnp.repeat(row_scales, BLOCK, axis=1)).astype(bf16)

    def picked(array):
        return jnp.stack(
            [mm(select, array[:, y * cols : (y + 1) * cols]).astype(bf16) for y in range(n_y)]
        )

    hq, wide = down_proj.shape[1:]
    units = hq // QUARTERS // PARTS
    joined = jnp.stack([gate_proj[0].T, up_proj[0].T, down_proj[0]])
    joined = joined.reshape(3, QUARTERS, PARTS, units, wide).transpose(2, 1, 0, 3, 4)
    along_x = [weights_along_x(joined[p]) for p in range(PARTS)]

    sent = jnp.concatenate([picked(x), picked(output_grad)], axis=1)
    sent, *along_x = lax.optimization_barrier((sent, *along_x))
    got = lax.all_to_all(sent, "y", split_axis=0, concat_axis=0, tiled=True)

    along_l = [weights_along_l(piece) for piece in along_x]
    got, *along_l = lax.optimization_barrier((got, *along_l))
    own = [weights_spread(piece) for piece in along_l]
    pieces = own + [shift(piece, "c", 1) for piece in own]
    place = jnp.stack([lax.axis_index("y"), lax.axis_index("c")]).astype(jnp.int32)

    total = n_y * n_ex
    at = jnp.arange(2 * total, dtype=jnp.int32)
    device, kind, source = at // (2 * n_y), at // n_y % 2, at % n_y
    to_send = one_hot_rows(source * (2 * n_ex) + kind * n_ex + device)
    kind, source, device = at // total, at // n_ex % n_y, at % n_ex
    to_split = one_hot_rows(device * (2 * n_y) + kind * n_y + source)

    mine = mm(to_send, got.reshape(2 * total, cols)).astype(bf16).reshape(n_ex, 2 * n_y, cols)
    there = lax.all_to_all(mine, EX, split_axis=0, concat_axis=0, tiled=True)
    rows = mm(to_split, there.reshape(2 * total, cols)).astype(bf16)

    parts = forward_parts(place, rows[:total], rows[total:], pieces, n_y)
    summed = parts[0].astype(f32)
    for k in range(1, n_y):
        summed = summed + shift(parts[k], "y", k).astype(f32)
    hidden = summed.shape[1] // 3
    acts = jnp.concatenate(
        swiglu_grads(summed[:, :hidden], summed[:, hidden : 2 * hidden], summed[:, 2 * hidden :]),
        axis=1,
    )
    acts = [acts] + [shift(acts, "y", k) for k in range(1, n_y)]
    part = backward_parts(place, acts, pieces)
    home = lax.all_to_all(
        part.reshape(total, 1, cols), ("y",) + EX, split_axis=0, concat_axis=0, tiled=True
    )
    high = weighting.astype(bf16)
    low = (weighting - high.astype(f32)).astype(bf16)
    return combined(high, low, home.reshape(n_y, n_ex, cols))


def solution(mesh):
    n_dp, n_ex = mesh.devices.shape
    fine = Mesh(
        mesh.devices.reshape(n_dp // 2, 2, QUARTERS, n_ex // QUARTERS**2, QUARTERS),
        ("y", "c", "x", "h", "l"),
    )
    tok = P(("y", "c", "x", "h", "l"), None)
    dp = ("y", "c")
    return jax.shard_map(
        per_device,
        mesh=fine,
        in_specs=(tok, tok, tok, tok, tok, P(EX, dp, None), P(EX, dp, None), P(EX, None, dp)),
        out_specs=tok,
        check_vma=False,
    )
```

```python
import jax
import jax.numpy as jnp
from jax import lax
from jax.experimental import pallas as pl
from jax.experimental.pallas import tpu as pltpu
from jax.sharding import Mesh, PartitionSpec as P

BLOCK = 128
CAP = 4
QUARTERS = 4

EX = ("x", "h", "l")
bf16 = jnp.bfloat16
f32 = jnp.float32


def mm(left, right):
    return jnp.dot(left, right, preferred_element_type=f32)


def mm_t(left, right):
    return lax.dot_general(left, right, (((1,), (1,)), ((), ())), preferred_element_type=f32)


def shift(array, axis, k):
    n = lax.axis_size(axis)
    return lax.ppermute(array, axis, [(i, (i + k) % n) for i in range(n)])


def swiglu_grads(gate_val, up_val, hidden_grad):
    sigmoid_gate = jax.nn.sigmoid(gate_val)
    gate_grad = hidden_grad * up_val * sigmoid_gate * (1.0 + gate_val * (1.0 - sigmoid_gate))
    up_grad = hidden_grad * gate_val * sigmoid_gate
    return gate_grad.astype(bf16), up_grad.astype(bf16)


def weight_copies(core, pieces, held, sems, kinds):
    half = len(pieces) // 2
    copies = [[] for _ in range(kinds)]
    for side in range(2):
        first = 0
        for n in range(side * half, side * half + half):
            groups = pieces[n].shape[0]
            for kind in range(kinds):
                target = held.at[core if side == 0 else 1 - core, kind, first : first + groups]
                copies[kind].append(
                    pltpu.make_async_copy(pieces[n].at[:, kind], target, sems.at[kind, n])
                )
            first += groups
    return copies


def forward_kernel(place, order_ref, there_ref, *refs):
    pieces, (out_ref, held, rows_held, sems) = refs[:-4], refs[-4:]
    copies = weight_copies(place[1], pieces, held, sems, 3)
    for group in copies:
        for copy in group:
            copy.start()
    n_y, rows, _ = out_ref.shape
    rows_held[...] = mm(order_ref[...], there_ref[...]).astype(bf16)
    x_ref, g_ref = rows_held.at[: n_y * rows], rows_held.at[n_y * rows :]
    _, _, groups, units, cols = held.shape
    span = QUARTERS * units
    for kind, rows_ref in enumerate((x_ref, x_ref, g_ref)):
        for copy in copies[kind]:
            copy.wait()
        for block in range(groups // QUARTERS):
            now = slice(block * QUARTERS, (block + 1) * QUARTERS)
            part = mm_t(rows_ref[:, :cols], held[0, kind, now].reshape(span, cols))
            part = part + mm_t(rows_ref[:, cols:], held[1, kind, now].reshape(span, cols))
            at = (kind * (groups // QUARTERS) + block) * span
            out_ref[:, :, at : at + span] = part.astype(bf16).reshape(n_y, rows, span)


def backward_kernel(place, *refs):
    acts, pieces = refs[:QUARTERS], refs[QUARTERS:-5]
    out_ref, held, acts_held, sems, act_sems = refs[-5:]
    copies = weight_copies(place[1], pieces, held, sems, 2)
    act_copies = [
        pltpu.make_async_copy(act, acts_held.at[(place[0] - k + QUARTERS) % QUARTERS], act_sems.at[k])
        for k, act in enumerate(acts)
    ]
    for copy in act_copies:
        copy.start()
    for group in copies:
        for copy in group:
            copy.start()
    for copy in act_copies:
        copy.wait()
    for group in copies:
        for copy in group:
            copy.wait()
    n_y, rows, width = acts_held.shape
    _, _, groups, units, cols = held.shape
    hidden = groups * units
    both = acts_held[...].reshape(n_y * rows, width)
    for half in range(2):
        part = mm(both[:, :hidden], held[half, 0].reshape(hidden, cols))
        part = part + mm(both[:, hidden:], held[half, 1].reshape(hidden, cols))
        out_ref[:, half] = part.astype(bf16)


ANY = pl.BlockSpec(memory_space=pl.ANY)
VMEM = pl.BlockSpec(memory_space=pltpu.VMEM)
SMEM = pl.BlockSpec(memory_space=pltpu.SMEM)
PARAMS = pltpu.CompilerParams(vmem_limit_bytes=40 * 1024 * 1024)


def held_shape(pieces, kinds):
    groups = sum(piece.shape[0] for piece in pieces) // 2
    return (2, kinds, groups) + pieces[0].shape[2:]


def forward_parts(place, order, there, pieces, n_y):
    both, width = there.shape
    total = both // 2
    held = held_shape(pieces, 3)
    hidden = held[2] * held[3]
    return pl.pallas_call(
        forward_kernel,
        out_shape=jax.ShapeDtypeStruct((n_y, total // n_y, 3 * hidden), bf16),
        in_specs=[SMEM, VMEM, VMEM] + [ANY] * len(pieces),
        out_specs=VMEM,
        scratch_shapes=[
            pltpu.VMEM(held, bf16),
            pltpu.VMEM((both, width), bf16),
            pltpu.SemaphoreType.DMA((3, len(pieces))),
        ],
        compiler_params=PARAMS,
        cost_estimate=pl.CostEstimate(
            flops=6 * total * width * hidden + 2 * both * both * width,
            bytes_accessed=6 * width * hidden,
            transcendentals=0,
        ),
    )(place, order, there, *pieces)


def backward_parts(place, acts, pieces):
    rows, double = acts[0].shape
    held = held_shape(pieces, 2)
    total, cols = QUARTERS * rows, held[4]
    return pl.pallas_call(
        backward_kernel,
        out_shape=jax.ShapeDtypeStruct((total, 2, cols), bf16),
        in_specs=[SMEM] + [ANY] * (QUARTERS + len(pieces)),
        out_specs=VMEM,
        scratch_shapes=[
            pltpu.VMEM(held, bf16),
            pltpu.VMEM((QUARTERS, rows, double), bf16),
            pltpu.SemaphoreType.DMA((2, len(pieces))),
            pltpu.SemaphoreType.DMA((QUARTERS,)),
        ],
        compiler_params=PARAMS,
        cost_estimate=pl.CostEstimate(
            flops=4 * total * double * cols,
            bytes_accessed=4 * double * cols,
            transcendentals=0,
        ),
    )(place, *acts, *pieces)


def combine_kernel(high_ref, low_ref, home_ref, out_ref):
    cols = home_ref.shape[2]
    for y in range(home_ref.shape[0]):
        total = mm(high_ref[...], home_ref[y]) + mm(low_ref[...], home_ref[y])
        out_ref[:, y * cols : (y + 1) * cols] = total.astype(bf16)


def combined(high, low, home):
    n_y, slots, cols = home.shape
    tokens = high.shape[0]
    return pl.pallas_call(
        combine_kernel,
        out_shape=jax.ShapeDtypeStruct((tokens, n_y * cols), bf16),
        in_specs=[VMEM] * 3,
        out_specs=VMEM,
        compiler_params=PARAMS,
        cost_estimate=pl.CostEstimate(
            flops=4 * tokens * slots * n_y * cols,
            bytes_accessed=4 * slots * n_y * cols,
            transcendentals=0,
        ),
    )(high, low, home)


def pick(array, index):
    return lax.dynamic_index_in_dim(array, index % QUARTERS, 0, keepdims=False)


def weights_along_x(joined):
    x = lax.axis_index("x")
    return [pick(joined, x)] + [shift(pick(joined, x + k), "x", k) for k in range(1, QUARTERS)]


def weights_along_l(along_x):
    x, l = lax.axis_index("x"), lax.axis_index("l")
    return jnp.stack(
        [pick(along_x, x - l + QUARTERS)]
        + [shift(pick(along_x, x - l - m + 2 * QUARTERS), "l", m) for m in range(1, QUARTERS)]
    )


def weights_spread(along_l):
    left, right = shift(along_l, "x", 1), shift(along_l, "x", -1)
    half = along_l.shape[0] // 2
    own = [along_l, left, right, shift(left[:half], "x", 1), shift(right[half:], "x", -1)]
    return own + [shift(piece, "c", 1) for piece in own]


def one_hot_rows(source):
    count = source.shape[0]
    return (source[:, None] == jnp.arange(count, dtype=jnp.int32)[None, :]).astype(bf16)


def per_device(
    input_rows, row_scales, output_grad, expert_ids, combine_weights, gate_proj, up_proj, down_proj
):
    tokens, width = input_rows.shape
    n_y, n_ex = lax.axis_size("y"), lax.axis_size(EX)
    window = n_ex // QUARTERS
    cols = width // n_y

    hq, wide = down_proj.shape[1:]
    joined = jnp.stack([gate_proj[0].T, up_proj[0].T, down_proj[0]])
    joined = joined.reshape(3, QUARTERS, hq // QUARTERS, wide).transpose(1, 0, 2, 3)

    hits = (expert_ids[:, :, None] == jnp.arange(window, dtype=jnp.int32)).astype(f32)
    member = jnp.sum(hits, axis=1)
    pick_weight = jnp.sum(combine_weights[:, :, None] * hits, axis=1)
    before = jnp.cumsum(member, axis=0) - member
    select = member[:, :, None] * (
        before[:, :, None] == jnp.arange(CAP, dtype=f32)
    ).astype(f32)

    def by_device(array):
        split = array.reshape(tokens, QUARTERS, window // QUARTERS, CAP)
        return split.transpose(0, 3, 2, 1).reshape(tokens, n_ex)

    weighting = by_device(select * pick_weight[:, :, None])
    select = by_device(select).T.astype(bf16)

    x = (input_rows.astype(f32) * jnp.repeat(row_scales, BLOCK, axis=1)).astype(bf16)

    def picked(array):
        return jnp.stack(
            [mm(select, array[:, y * cols : (y + 1) * cols]).astype(bf16) for y in range(n_y)]
        )

    sent = jnp.concatenate([picked(x), picked(output_grad)], axis=1)
    along_x = weights_along_x(joined)
    sent, *along_x = lax.optimization_barrier((sent, *along_x))
    got = lax.all_to_all(sent, "y", split_axis=0, concat_axis=0, tiled=True)

    along_l = weights_along_l(jnp.stack(along_x))
    got, along_l = lax.optimization_barrier((got, along_l))
    pieces = weights_spread(along_l)
    place = jnp.stack([lax.axis_index("y"), lax.axis_index("c")]).astype(jnp.int32)

    total = n_y * n_ex
    at = jnp.arange(2 * total, dtype=jnp.int32)
    device, kind, source = at // (2 * n_y), at // n_y % 2, at % n_y
    to_send = one_hot_rows(source * (2 * n_ex) + kind * n_ex + device)
    kind, source, device = at // total, at // n_ex % n_y, at % n_ex
    to_split = one_hot_rows(device * (2 * n_y) + kind * n_y + source)

    mine = mm(to_send, got.reshape(2 * total, cols)).astype(bf16).reshape(n_ex, 2 * n_y, cols)
    there = lax.all_to_all(mine, EX, split_axis=0, concat_axis=0, tiled=True)
    parts = forward_parts(place, to_split, there.reshape(2 * total, cols), pieces, n_y)
    parts = lax.all_to_all(parts, "y", split_axis=0, concat_axis=0, tiled=True)
    summed = jnp.sum(parts.astype(f32), axis=0)
    hidden = summed.shape[1] // 3
    acts = jnp.concatenate(
        swiglu_grads(summed[:, :hidden], summed[:, hidden : 2 * hidden], summed[:, 2 * hidden :]),
        axis=1,
    )
    acts = [acts] + [shift(acts, "y", k) for k in range(1, n_y)]
    part = backward_parts(place, acts, pieces)
    home = lax.all_to_all(
        part, ("y",) + EX, split_axis=0, concat_axis=0, tiled=True
    )
    high = weighting.astype(bf16)
    low = (weighting - high.astype(f32)).astype(bf16)
    return combined(high, low, home.reshape(n_y, n_ex, cols))


def solution(mesh):
    n_dp, n_ex = mesh.devices.shape
    fine = Mesh(
        mesh.devices.reshape(n_dp // 2, 2, QUARTERS, n_ex // QUARTERS**2, QUARTERS),
        ("y", "c", "x", "h", "l"),
    )
    tok = P(("y", "c", "x", "h", "l"), None)
    dp = ("y", "c")
    return jax.shard_map(
        per_device,
        mesh=fine,
        in_specs=(tok, tok, tok, tok, tok, P(EX, dp, None), P(EX, dp, None), P(EX, None, dp)),
        out_specs=tok,
        check_vma=False,
    )
```

```python
import jax
import jax.numpy as jnp
from jax import lax
from jax.experimental import pallas as pl
from jax.experimental.pallas import tpu as pltpu
from jax.sharding import Mesh, PartitionSpec as P

BLOCK = 128
CAP = 4
QUARTERS = 4

EX = ("x", "h", "l")
bf16 = jnp.bfloat16
f32 = jnp.float32


def mm(left, right):
    return jnp.dot(left, right, preferred_element_type=f32)


def mm_t(left, right):
    return lax.dot_general(left, right, (((1,), (1,)), ((), ())), preferred_element_type=f32)


def shift(array, axis, k):
    n = lax.axis_size(axis)
    return lax.ppermute(array, axis, [(i, (i + k) % n) for i in range(n)])


def swiglu_grads(gate_val, up_val, hidden_grad):
    sigmoid_gate = jax.nn.sigmoid(gate_val)
    gate_grad = hidden_grad * up_val * sigmoid_gate * (1.0 + gate_val * (1.0 - sigmoid_gate))
    up_grad = hidden_grad * gate_val * sigmoid_gate
    return gate_grad.astype(bf16), up_grad.astype(bf16)


def weight_copies(core, pieces, held, sems, kinds):
    half = len(pieces) // 2
    copies = [[] for _ in range(kinds)]
    for side in range(2):
        first = 0
        for n in range(side * half, side * half + half):
            groups = pieces[n].shape[0]
            for kind in range(kinds):
                target = held.at[core if side == 0 else 1 - core, kind, first : first + groups]
                copies[kind].append(
                    pltpu.make_async_copy(pieces[n].at[:, kind], target, sems.at[kind, n])
                )
            first += groups
    return copies


def forward_kernel(place, order_ref, there_ref, *refs):
    pieces, (out_ref, held, rows_held, sems) = refs[:-4], refs[-4:]
    copies = weight_copies(place[1], pieces, held, sems, 3)
    for group in copies:
        for copy in group:
            copy.start()
    n_y, rows, _ = out_ref.shape
    rows_held[...] = mm(order_ref[...], there_ref[...]).astype(bf16)
    x_ref, g_ref = rows_held.at[: n_y * rows], rows_held.at[n_y * rows :]
    _, _, groups, units, cols = held.shape
    span = QUARTERS * units
    for kind, rows_ref in enumerate((x_ref, x_ref, g_ref)):
        for copy in copies[kind]:
            copy.wait()
        for block in range(groups // QUARTERS):
            now = slice(block * QUARTERS, (block + 1) * QUARTERS)
            part = mm_t(rows_ref[:, :cols], held[0, kind, now].reshape(span, cols))
            part = part + mm_t(rows_ref[:, cols:], held[1, kind, now].reshape(span, cols))
            at = (kind * (groups // QUARTERS) + block) * span
            out_ref[:, :, at : at + span] = part.astype(bf16).reshape(n_y, rows, span)


def backward_kernel(place, acts_ref, *refs):
    pieces, (out_ref, held, sems) = refs[:-3], refs[-3:]
    copies = weight_copies(place[1], pieces, held, sems, 2)
    for group in copies:
        for copy in group:
            copy.start()
    n_y, rows, width = acts_ref.shape
    _, _, groups, units, cols = held.shape
    hidden = groups * units
    both = acts_ref[...].reshape(n_y * rows, width)
    for group in copies:
        for copy in group:
            copy.wait()
    for half in range(2):
        part = mm(both[:, :hidden], held[half, 0].reshape(hidden, cols))
        part = part + mm(both[:, hidden:], held[half, 1].reshape(hidden, cols))
        out_ref[:, half] = part.astype(bf16)


ANY = pl.BlockSpec(memory_space=pl.ANY)
VMEM = pl.BlockSpec(memory_space=pltpu.VMEM)
SMEM = pl.BlockSpec(memory_space=pltpu.SMEM)
PARAMS = pltpu.CompilerParams(vmem_limit_bytes=40 * 1024 * 1024)


def held_shape(pieces, kinds):
    groups = sum(piece.shape[0] for piece in pieces) // 2
    return (2, kinds, groups) + pieces[0].shape[2:]


def forward_parts(place, order, there, pieces, n_y):
    both, width = there.shape
    total = both // 2
    held = held_shape(pieces, 3)
    hidden = held[2] * held[3]
    return pl.pallas_call(
        forward_kernel,
        out_shape=jax.ShapeDtypeStruct((n_y, total // n_y, 3 * hidden), bf16),
        in_specs=[SMEM, VMEM, VMEM] + [ANY] * len(pieces),
        out_specs=VMEM,
        scratch_shapes=[
            pltpu.VMEM(held, bf16),
            pltpu.VMEM((both, width), bf16),
            pltpu.SemaphoreType.DMA((3, len(pieces))),
        ],
        compiler_params=PARAMS,
        cost_estimate=pl.CostEstimate(
            flops=6 * total * width * hidden + 2 * both * both * width,
            bytes_accessed=6 * width * hidden,
            transcendentals=0,
        ),
    )(place, order, there, *pieces)


def backward_parts(place, acts, pieces):
    n_y, rows, double = acts.shape
    held = held_shape(pieces, 2)
    total, cols = n_y * rows, held[4]
    return pl.pallas_call(
        backward_kernel,
        out_shape=jax.ShapeDtypeStruct((total, 2, cols), bf16),
        in_specs=[SMEM, VMEM] + [ANY] * len(pieces),
        out_specs=VMEM,
        scratch_shapes=[pltpu.VMEM(held, bf16), pltpu.SemaphoreType.DMA((2, len(pieces)))],
        compiler_params=PARAMS,
        cost_estimate=pl.CostEstimate(
            flops=4 * total * double * cols,
            bytes_accessed=4 * double * cols,
            transcendentals=0,
        ),
    )(place, acts, *pieces)


def combine_kernel(high_ref, low_ref, home_ref, out_ref):
    cols = home_ref.shape[2]
    for y in range(home_ref.shape[0]):
        total = mm(high_ref[...], home_ref[y]) + mm(low_ref[...], home_ref[y])
        out_ref[:, y * cols : (y + 1) * cols] = total.astype(bf16)


def combined(high, low, home):
    n_y, slots, cols = home.shape
    tokens = high.shape[0]
    return pl.pallas_call(
        combine_kernel,
        out_shape=jax.ShapeDtypeStruct((tokens, n_y * cols), bf16),
        in_specs=[VMEM] * 3,
        out_specs=VMEM,
        compiler_params=PARAMS,
        cost_estimate=pl.CostEstimate(
            flops=4 * tokens * slots * n_y * cols,
            bytes_accessed=4 * slots * n_y * cols,
            transcendentals=0,
        ),
    )(high, low, home)


def pick(array, index):
    return lax.dynamic_index_in_dim(array, index % QUARTERS, 0, keepdims=False)


def weights_along_x(joined):
    x = lax.axis_index("x")
    return [pick(joined, x)] + [shift(pick(joined, x + k), "x", k) for k in range(1, QUARTERS)]


def weights_along_l(along_x):
    x, l = lax.axis_index("x"), lax.axis_index("l")
    return jnp.stack(
        [pick(along_x, x - l + QUARTERS)]
        + [shift(pick(along_x, x - l - m + 2 * QUARTERS), "l", m) for m in range(1, QUARTERS)]
    )


def weights_spread(along_l):
    left, right = shift(along_l, "x", 1), shift(along_l, "x", -1)
    half = along_l.shape[0] // 2
    own = [along_l, left, right, shift(left[:half], "x", 1), shift(right[half:], "x", -1)]
    return own + [shift(piece, "c", 1) for piece in own]


def one_hot_rows(source):
    count = source.shape[0]
    return (source[:, None] == jnp.arange(count, dtype=jnp.int32)[None, :]).astype(bf16)


def per_device(
    input_rows, row_scales, output_grad, expert_ids, combine_weights, gate_proj, up_proj, down_proj
):
    tokens, width = input_rows.shape
    n_y, n_ex = lax.axis_size("y"), lax.axis_size(EX)
    window = n_ex // QUARTERS
    cols = width // n_y

    hq, wide = down_proj.shape[1:]
    joined = jnp.stack([gate_proj[0].T, up_proj[0].T, down_proj[0]])
    joined = joined.reshape(3, QUARTERS, hq // QUARTERS, wide).transpose(1, 0, 2, 3)

    hits = (expert_ids[:, :, None] == jnp.arange(window, dtype=jnp.int32)).astype(f32)
    member = jnp.sum(hits, axis=1)
    pick_weight = jnp.sum(combine_weights[:, :, None] * hits, axis=1)
    before = jnp.cumsum(member, axis=0) - member
    select = member[:, :, None] * (
        before[:, :, None] == jnp.arange(CAP, dtype=f32)
    ).astype(f32)

    def by_device(array):
        split = array.reshape(tokens, QUARTERS, window // QUARTERS, CAP)
        return split.transpose(0, 3, 2, 1).reshape(tokens, n_ex)

    weighting = by_device(select * pick_weight[:, :, None])
    select = by_device(select).T.astype(bf16)

    x = (input_rows.astype(f32) * jnp.repeat(row_scales, BLOCK, axis=1)).astype(bf16)

    def picked(array):
        return jnp.stack(
            [mm(select, array[:, y * cols : (y + 1) * cols]).astype(bf16) for y in range(n_y)]
        )

    sent = jnp.concatenate([picked(x), picked(output_grad)], axis=1)
    along_x = weights_along_x(joined)
    sent, *along_x = lax.optimization_barrier((sent, *along_x))
    got = lax.all_to_all(sent, "y", split_axis=0, concat_axis=0, tiled=True)

    along_l = weights_along_l(jnp.stack(along_x))
    got, along_l = lax.optimization_barrier((got, along_l))
    pieces = weights_spread(along_l)
    place = jnp.stack([lax.axis_index("y"), lax.axis_index("c")]).astype(jnp.int32)

    total = n_y * n_ex
    at = jnp.arange(2 * total, dtype=jnp.int32)
    device, kind, source = at // (2 * n_y), at // n_y % 2, at % n_y
    to_send = one_hot_rows(source * (2 * n_ex) + kind * n_ex + device)
    kind, source, device = at // total, at // n_ex % n_y, at % n_ex
    to_split = one_hot_rows(device * (2 * n_y) + kind * n_y + source)

    mine = mm(to_send, got.reshape(2 * total, cols)).astype(bf16).reshape(n_ex, 2 * n_y, cols)
    there = lax.all_to_all(mine, EX, split_axis=0, concat_axis=0, tiled=True)
    parts = forward_parts(place, to_split, there.reshape(2 * total, cols), pieces, n_y)
    parts = lax.all_to_all(parts, "y", split_axis=0, concat_axis=0, tiled=True)
    summed = jnp.sum(parts.astype(f32), axis=0)
    hidden = summed.shape[1] // 3
    acts = jnp.concatenate(
        swiglu_grads(summed[:, :hidden], summed[:, hidden : 2 * hidden], summed[:, 2 * hidden :]),
        axis=1,
    )
    acts = jnp.broadcast_to(acts[None], (n_y,) + acts.shape)
    acts = lax.all_to_all(acts, "y", split_axis=0, concat_axis=0, tiled=True)
    part = backward_parts(place, acts, pieces)
    home = lax.all_to_all(
        part, ("y",) + EX, split_axis=0, concat_axis=0, tiled=True
    )
    high = weighting.astype(bf16)
    low = (weighting - high.astype(f32)).astype(bf16)
    return combined(high, low, home.reshape(n_y, n_ex, cols))


def solution(mesh):
    n_dp, n_ex = mesh.devices.shape
    fine = Mesh(
        mesh.devices.reshape(n_dp // 2, 2, QUARTERS, n_ex // QUARTERS**2, QUARTERS),
        ("y", "c", "x", "h", "l"),
    )
    tok = P(("y", "c", "x", "h", "l"), None)
    dp = ("y", "c")
    return jax.shard_map(
        per_device,
        mesh=fine,
        in_specs=(tok, tok, tok, tok, tok, P(EX, dp, None), P(EX, dp, None), P(EX, None, dp)),
        out_specs=tok,
        check_vma=False,
    )
```

```python
import jax
import jax.numpy as jnp
from jax import lax
from jax.experimental import pallas as pl
from jax.experimental.pallas import tpu as pltpu
from jax.sharding import Mesh, PartitionSpec as P

BLOCK = 128
CAP = 4
QUARTERS = 4

EX = ("x", "h", "l")
bf16 = jnp.bfloat16
f32 = jnp.float32


def mm(left, right):
    return jnp.dot(left, right, preferred_element_type=f32)


def mm_t(left, right):
    return lax.dot_general(left, right, (((1,), (1,)), ((), ())), preferred_element_type=f32)


def shift(array, axis, k):
    n = lax.axis_size(axis)
    return lax.ppermute(array, axis, [(i, (i + k) % n) for i in range(n)])


def swiglu_grads(gate_val, up_val, hidden_grad):
    sigmoid_gate = jax.nn.sigmoid(gate_val)
    gate_grad = hidden_grad * up_val * sigmoid_gate * (1.0 + gate_val * (1.0 - sigmoid_gate))
    up_grad = hidden_grad * gate_val * sigmoid_gate
    return gate_grad.astype(bf16), up_grad.astype(bf16)


def weight_copies(core, pieces, held, sems, kinds):
    half = len(pieces) // 2
    copies = [[] for _ in range(kinds)]
    for side in range(2):
        first = 0
        for n in range(side * half, side * half + half):
            groups = pieces[n].shape[0]
            for kind in range(kinds):
                target = held.at[core if side == 0 else 1 - core, kind, first : first + groups]
                copies[kind].append(
                    pltpu.make_async_copy(pieces[n].at[:, kind], target, sems.at[kind, n])
                )
            first += groups
    return copies


def forward_kernel(place, order_ref, there_ref, *refs):
    pieces, (out_ref, held, rows_held, sems) = refs[:-4], refs[-4:]
    copies = weight_copies(place[1], pieces, held, sems, 3)
    for group in copies:
        for copy in group:
            copy.start()
    n_y, rows, _ = out_ref.shape
    rows_held[...] = mm(order_ref[...], there_ref[...]).astype(bf16)
    x_ref, g_ref = rows_held.at[: n_y * rows], rows_held.at[n_y * rows :]
    _, _, groups, units, cols = held.shape
    span = QUARTERS * units
    for kind, rows_ref in enumerate((x_ref, x_ref, g_ref)):
        for copy in copies[kind]:
            copy.wait()
        for block in range(groups // QUARTERS):
            now = slice(block * QUARTERS, (block + 1) * QUARTERS)
            part = mm_t(rows_ref[:, :cols], held[0, kind, now].reshape(span, cols))
            part = part + mm_t(rows_ref[:, cols:], held[1, kind, now].reshape(span, cols))
            at = (kind * (groups // QUARTERS) + block) * span
            out_ref[:, :, at : at + span] = part.astype(bf16).reshape(n_y, rows, span)


def backward_kernel(place, acts_ref, *refs):
    pieces, (out_ref, held, sems) = refs[:-3], refs[-3:]
    copies = weight_copies(place[1], pieces, held, sems, 2)
    for group in copies:
        for copy in group:
            copy.start()
    n_y, rows, width = acts_ref.shape
    _, _, groups, units, cols = held.shape
    hidden = groups * units
    both = acts_ref[...].reshape(n_y * rows, width)
    for group in copies:
        for copy in group:
            copy.wait()
    for half in range(2):
        part = mm(both[:, :hidden], held[half, 0].reshape(hidden, cols))
        part = part + mm(both[:, hidden:], held[half, 1].reshape(hidden, cols))
        out_ref[:, half] = part.astype(bf16)


ANY = pl.BlockSpec(memory_space=pl.ANY)
VMEM = pl.BlockSpec(memory_space=pltpu.VMEM)
SMEM = pl.BlockSpec(memory_space=pltpu.SMEM)
PARAMS = pltpu.CompilerParams(vmem_limit_bytes=40 * 1024 * 1024)


def held_shape(pieces, kinds):
    groups = sum(piece.shape[0] for piece in pieces) // 2
    return (2, kinds, groups) + pieces[0].shape[2:]


def forward_parts(place, order, there, pieces, n_y):
    both, width = there.shape
    total = both // 2
    held = held_shape(pieces, 3)
    hidden = held[2] * held[3]
    return pl.pallas_call(
        forward_kernel,
        out_shape=jax.ShapeDtypeStruct((n_y, total // n_y, 3 * hidden), bf16),
        in_specs=[SMEM, VMEM, VMEM] + [ANY] * len(pieces),
        out_specs=VMEM,
        scratch_shapes=[
            pltpu.VMEM(held, bf16),
            pltpu.VMEM((both, width), bf16),
            pltpu.SemaphoreType.DMA((3, len(pieces))),
        ],
        compiler_params=PARAMS,
        cost_estimate=pl.CostEstimate(
            flops=6 * total * width * hidden + 2 * both * both * width,
            bytes_accessed=6 * width * hidden,
            transcendentals=0,
        ),
    )(place, order, there, *pieces)


def backward_parts(place, acts, pieces):
    n_y, rows, double = acts.shape
    held = held_shape(pieces, 2)
    total, cols = n_y * rows, held[4]
    return pl.pallas_call(
        backward_kernel,
        out_shape=jax.ShapeDtypeStruct((total, 2, cols), bf16),
        in_specs=[SMEM, VMEM] + [ANY] * len(pieces),
        out_specs=VMEM,
        scratch_shapes=[pltpu.VMEM(held, bf16), pltpu.SemaphoreType.DMA((2, len(pieces)))],
        compiler_params=PARAMS,
        cost_estimate=pl.CostEstimate(
            flops=4 * total * double * cols,
            bytes_accessed=4 * double * cols,
            transcendentals=0,
        ),
    )(place, acts, *pieces)


def combine_kernel(high_ref, low_ref, home_ref, out_ref):
    cols = home_ref.shape[2]
    for y in range(home_ref.shape[0]):
        total = mm(high_ref[...], home_ref[y]) + mm(low_ref[...], home_ref[y])
        out_ref[:, y * cols : (y + 1) * cols] = total.astype(bf16)


def combined(high, low, home):
    n_y, slots, cols = home.shape
    tokens = high.shape[0]
    return pl.pallas_call(
        combine_kernel,
        out_shape=jax.ShapeDtypeStruct((tokens, n_y * cols), bf16),
        in_specs=[VMEM] * 3,
        out_specs=VMEM,
        compiler_params=PARAMS,
        cost_estimate=pl.CostEstimate(
            flops=4 * tokens * slots * n_y * cols,
            bytes_accessed=4 * slots * n_y * cols,
            transcendentals=0,
        ),
    )(high, low, home)


def pick(array, index):
    return lax.dynamic_index_in_dim(array, index % QUARTERS, 0, keepdims=False)


def weights_along_x(joined):
    x = lax.axis_index("x")
    return [pick(joined, x)] + [shift(pick(joined, x + k), "x", k) for k in range(1, QUARTERS)]


def weights_along_l(along_x):
    x, l = lax.axis_index("x"), lax.axis_index("l")
    return jnp.stack(
        [pick(along_x, x - l + QUARTERS)]
        + [shift(pick(along_x, x - l - m + 2 * QUARTERS), "l", m) for m in range(1, QUARTERS)]
    )


def weights_spread(along_l):
    left, right = shift(along_l, "x", 1), shift(along_l, "x", -1)
    half = along_l.shape[0] // 2
    own = [along_l, left, right, shift(left[:half], "x", 1), shift(right[half:], "x", -1)]
    return own + [shift(piece, "c", 1) for piece in own]


def one_hot_rows(source):
    count = source.shape[0]
    return (source[:, None] == jnp.arange(count, dtype=jnp.int32)[None, :]).astype(bf16)


def per_device(
    input_rows, row_scales, output_grad, expert_ids, combine_weights, gate_proj, up_proj, down_proj
):
    tokens, width = input_rows.shape
    n_y, n_ex = lax.axis_size("y"), lax.axis_size(EX)
    window = n_ex // QUARTERS
    cols = width // n_y

    hq, wide = down_proj.shape[1:]
    joined = jnp.stack([gate_proj[0].T, up_proj[0].T, down_proj[0]])
    joined = joined.reshape(3, QUARTERS, hq // QUARTERS, wide).transpose(1, 0, 2, 3)

    hits = (expert_ids[:, :, None] == jnp.arange(window, dtype=jnp.int32)).astype(f32)
    member = jnp.sum(hits, axis=1)
    pick_weight = jnp.sum(combine_weights[:, :, None] * hits, axis=1)
    before = jnp.cumsum(member, axis=0) - member
    select = member[:, :, None] * (
        before[:, :, None] == jnp.arange(CAP, dtype=f32)
    ).astype(f32)

    def by_device(array):
        split = array.reshape(tokens, QUARTERS, window // QUARTERS, CAP)
        return split.transpose(0, 3, 2, 1).reshape(tokens, n_ex)

    weighting = by_device(select * pick_weight[:, :, None])
    select = by_device(select).T.astype(bf16)

    x = (input_rows.astype(f32) * jnp.repeat(row_scales, BLOCK, axis=1)).astype(bf16)

    def picked(array):
        return jnp.stack(
            [mm(select, array[:, y * cols : (y + 1) * cols]).astype(bf16) for y in range(n_y)]
        )

    sent = jnp.concatenate([picked(x), picked(output_grad)], axis=1)
    along_x = weights_along_x(joined)
    sent, *along_x = lax.optimization_barrier((sent, *along_x))
    got = lax.all_to_all(sent, "y", split_axis=0, concat_axis=0, tiled=True)

    along_l = weights_along_l(jnp.stack(along_x))
    place = jnp.stack([lax.axis_index("y"), lax.axis_index("c")]).astype(jnp.int32)

    total = n_y * n_ex
    at = jnp.arange(2 * total, dtype=jnp.int32)
    device, kind, source = at // (2 * n_y), at // n_y % 2, at % n_y
    to_send = one_hot_rows(source * (2 * n_ex) + kind * n_ex + device)
    kind, source, device = at // total, at // n_ex % n_y, at % n_ex
    to_split = one_hot_rows(device * (2 * n_y) + kind * n_y + source)

    mine = mm(to_send, got.reshape(2 * total, cols)).astype(bf16).reshape(n_ex, 2 * n_y, cols)
    mine, along_l = lax.optimization_barrier((mine, along_l))
    pieces = weights_spread(along_l)
    there = lax.all_to_all(mine, EX, split_axis=0, concat_axis=0, tiled=True)
    parts = forward_parts(place, to_split, there.reshape(2 * total, cols), pieces, n_y)
    parts = lax.all_to_all(parts, "y", split_axis=0, concat_axis=0, tiled=True)
    summed = jnp.sum(parts.astype(f32), axis=0)
    hidden = summed.shape[1] // 3
    acts = jnp.concatenate(
        swiglu_grads(summed[:, :hidden], summed[:, hidden : 2 * hidden], summed[:, 2 * hidden :]),
        axis=1,
    )
    acts = jnp.broadcast_to(acts[None], (n_y,) + acts.shape)
    acts = lax.all_to_all(acts, "y", split_axis=0, concat_axis=0, tiled=True)
    part = backward_parts(place, acts, pieces)
    home = lax.all_to_all(
        part, ("y",) + EX, split_axis=0, concat_axis=0, tiled=True
    )
    high = weighting.astype(bf16)
    low = (weighting - high.astype(f32)).astype(bf16)
    return combined(high, low, home.reshape(n_y, n_ex, cols))


def solution(mesh):
    n_dp, n_ex = mesh.devices.shape
    fine = Mesh(
        mesh.devices.reshape(n_dp // 2, 2, QUARTERS, n_ex // QUARTERS**2, QUARTERS),
        ("y", "c", "x", "h", "l"),
    )
    tok = P(("y", "c", "x", "h", "l"), None)
    dp = ("y", "c")
    return jax.shard_map(
        per_device,
        mesh=fine,
        in_specs=(tok, tok, tok, tok, tok, P(EX, dp, None), P(EX, dp, None), P(EX, None, dp)),
        out_specs=tok,
        check_vma=False,
    )
```
